256 devices in a mesh: tile: 128 (over x, z, y), tm: 2 (over core).
Axes of the slice: x: 4, y: 4, z: 8, core: 2. Of those that a mesh axis runs over, the one named last changes fastest.
Arguments:
- clip_frames: bfloat16 [8, 1024, 6144], P('tm', 'tile'), may hold values from -6 to 6
- first_gain: float32 [96], replicated, may hold values from 0.1 to 1.9
- first_weight: bfloat16 [3, 3, 288, 96], replicated, may hold values from -0.125 to 0.125
- second_gain: float32 [96], replicated, may hold values from 0.1 to 1.9
- second_weight: bfloat16 [3, 3, 288, 96], replicated, may hold values from -0.125 to 0.125
- live_widths: int32 [128], P('tile'), may hold values from 32 to 64, as said below
- band_links: int32 [128, 2], P('tile'), may hold values from 0 to 1, as said below
Outputs:
- encoded: bfloat16 [8, 1024, 6144], P('tm', 'tile')
The draws below stay inside these ranges and needn't reach their ends.
Inputs may be any that keep to these rules, and one draw needn't show every extreme that they name: `live_widths`: the bands of one video are consecutive; all bands of a video have the same live width, one of 32, 48 and 64, and each of these occurs in every draw. band_links[b,1] equals band_links[b+1,0]; band_links[0,0] and the last band's column 1 are 0.
All inputs are finite; a program needn't handle non-finite values.
Results may differ from the reference program's by a relative error of at most 0.004.
Values may be sent and summed in bfloat16 or wider, within the bound.
No kernel may reach another device: no remote copies, remote signals or barrier semaphores. Data moves between devices by JAX's collectives and lax.ppermute only.
A program may use at most 64 MiB of HBM per device.

```python
import jax
import jax.numpy as jnp
from jax import lax

C = 96
BH = 8
BW = 64
TILES = 128
FRAMES = 8
ROWS = 1024
WIDE = 6144


def segment_plan(key):
    start_key, bucket_key, order_key = jax.random.split(key, 3)
    starts = jax.random.randint(start_key, (TILES,), 0, 4) == 0
    quarter = TILES // 4
    middle = TILES // 2
    late = 3 * TILES // 4
    starts = starts.at[0].set(True).at[quarter].set(True).at[late].set(True)
    starts = starts.at[middle].set(False).at[middle + 1].set(False)
    segment = jnp.cumsum(starts.astype(jnp.int32)) - 1
    buckets = jax.random.randint(bucket_key, (TILES,), 0, 3)
    order = jax.random.permutation(order_key, 3)
    buckets = buckets.at[segment[0]].set(order[0]).at[segment[quarter]].set(order[1]).at[segment[late]].set(order[2])
    widths = BW // 2 + buckets[segment] * (BW // 4)
    above_link = 1 - starts.astype(jnp.int32)
    below_link = jnp.concatenate([above_link[1:], jnp.zeros((1,), jnp.int32)])
    return (widths.astype(jnp.int32), jnp.stack([above_link, below_link], axis=1).astype(jnp.int32))


def draw_live_widths(key, part):
    return segment_plan(key)[0]


def draw_band_links(key, part):
    return segment_plan(key)[1]


def levels(rng, extent, cuts, smallest, top_value):
    def one(dim, parts):
        heights = jax.random.uniform(jax.random.fold_in(jax.random.fold_in(rng, 6), dim), (parts,), jnp.float32, smallest / len(cuts), top_value / len(cuts))
        return jnp.repeat(jnp.exp(heights), extent[dim] // parts).reshape((-1,) + (1,) * (len(extent) - dim - 1))

    gain = one(*cuts[0])
    for cut in cuts[1:]:
        gain = gain * one(*cut)
    return gain


def normal_values(rng, shape, scale, bound, cuts=(), dtype=jnp.bfloat16):
    factor_of = levels(rng, shape, cuts, -0.22, 0.18) if cuts else 1.0
    array = jax.random.normal(rng, shape, jnp.float32) * scale * factor_of
    return jnp.minimum(jnp.maximum(array, -bound), bound).astype(dtype)


def setup_inputs(seed: int = 0) -> dict:
    seeds = jax.random.split(jax.random.key(seed), 8)
    clip_frames = normal_values(seeds[0], (FRAMES, ROWS, WIDE), 1.0, 6.0, ((0, 2), (1, 128)))
    first_gain = jnp.clip(1.0 + 0.18 * jax.random.normal(seeds[1], (C,), jnp.float32), 0.1, 1.9)
    first_weight = normal_values(seeds[2], (3, 3, 3 * C, C), (27 * C) ** -0.5, 0.125)
    second_gain = jnp.clip(1.0 + 0.18 * jax.random.normal(seeds[3], (C,), jnp.float32), 0.1, 1.9)
    second_weight = normal_values(seeds[4], (3, 3, 3 * C, C), (27 * C) ** -0.5, 0.125)
    live_widths = draw_live_widths(jax.random.fold_in(seeds[7], 71), 0)
    band_links = draw_band_links(jax.random.fold_in(seeds[7], 71), 0)
    return dict(clip_frames=clip_frames, first_gain=first_gain, first_weight=first_weight, second_gain=second_gain, second_weight=second_weight, live_widths=live_widths, band_links=band_links)


def settle(values, gain_vec):
    mean_sq = lax.optimization_barrier(jnp.mean(values * values, axis=-1, keepdims=True))
    return jax.nn.silu(values * lax.rsqrt(mean_sq + 1e-06) * gain_vec)

def convolve(padded, weight):
    frames_out = padded.shape[0] - 2
    rows_out = padded.shape[1] - 2
    cols_out = padded.shape[2]
    channels = padded.shape[3]
    widened = jnp.pad(padded, ((0, 0), (0, 0), (1, 1), (0, 0)))
    accumulated = jnp.zeros((frames_out * rows_out * cols_out, channels), jnp.float32)
    for tap_t in range(3):
        for tap_h in range(3):
            window_slab = widened[tap_t:tap_t + frames_out, tap_h:tap_h + rows_out]
            tap_cols = jnp.concatenate([window_slab[:, :, tap_w:tap_w + cols_out] for tap_w in range(3)], axis=-1)
            accumulated = accumulated + jnp.dot(tap_cols.reshape(-1, 3 * channels), weight[tap_t, tap_h], preferred_element_type=jnp.float32)
    return accumulated.reshape(frames_out, rows_out, cols_out, channels)

def band_conv(hidden, weight, band_links):
    zero_band = jnp.zeros_like(hidden[:1, :, :1])
    link_above = band_links[:, 0].astype(jnp.bfloat16)[:, None, None, None, None]
    link_below = band_links[:, 1].astype(jnp.bfloat16)[:, None, None, None, None]
    from_above = jnp.concatenate([zero_band, hidden[:-1, :, -1:]], axis=0) * link_above
    from_below = jnp.concatenate([hidden[1:, :, :1], zero_band], axis=0) * link_below
    rowed = jnp.concatenate([from_above, hidden, from_below], axis=2)
    timed = jnp.pad(rowed, ((0, 0), (2, 0), (0, 0), (0, 0), (0, 0)))
    return lax.map(lambda single: convolve(single, weight), timed)

def reference(clip_frames, first_gain, first_weight, second_gain, second_weight, live_widths, band_links):
    frame_count = clip_frames.shape[0]
    bands = clip_frames.reshape(frame_count, TILES, BH, BW, C).transpose(1, 0, 2, 3, 4)
    column_mask = (jnp.arange(BW)[None, :] < live_widths[:, None]).astype(jnp.float32)[:, None, None, :, None]
    source = bands.astype(jnp.float32)
    first_hidden = (settle(source, first_gain) * column_mask).astype(jnp.bfloat16)
    first_out = band_conv(first_hidden, first_weight, band_links)
    second_hidden = (settle(first_out, second_gain) * column_mask).astype(jnp.bfloat16)
    second_out = band_conv(second_hidden, second_weight, band_links)
    encoded = ((source + second_out) * column_mask).astype(jnp.bfloat16)
    return encoded.transpose(1, 0, 2, 3, 4).reshape(frame_count, TILES * BH, BW * C)
```

```python
import jax
import jax.numpy as jnp
from jax import lax
from jax.experimental import pallas as pl
from jax.experimental.pallas import tpu as pltpu
from jax.sharding import PartitionSpec as P

C = 96
L = 128
BW = 64
BF = jnp.bfloat16
F32 = jnp.float32
VM = pltpu.VMEM
vmem = pl.BlockSpec(memory_space=pltpu.VMEM)
smem = pl.BlockSpec(memory_space=pltpu.SMEM)
PARAMS = pltpu.CompilerParams(vmem_limit_bytes=32 * 1024 * 1024)


def settle(x, half_gain, mask):
    ms = jnp.sum(x * x, axis=-1, keepdims=True) * (1.0 / C)
    v = x * (lax.rsqrt(ms + 1e-6) * mask) * half_gain
    return v + v * jnp.tanh(v)


def column_mask(widths):
    return (lax.broadcasted_iota(jnp.int32, (BW, 1), 0) < widths[0]).astype(F32)


def half_gain_of(gain):
    g = gain[...] * 0.5
    return jnp.concatenate([g, jnp.zeros((1, L - C), F32)], axis=1)


def spread(frame, scratch):
    pad = jnp.zeros((8, L - C), F32)
    for w in range(BW):
        piece = jnp.concatenate([frame[:, w * C : (w + 1) * C], pad], axis=1)
        scratch[pl.ds(w, 8, stride=BW), :] = piece


def shifts(h):
    row = lax.broadcasted_iota(jnp.int32, (BW, 1), 0)
    left = jnp.where(row == 0, 0.0, pltpu.roll(h, 1, 0))
    right = jnp.where(row == BW - 1, 0.0, pltpu.roll(h, BW - 1, 0))
    return left.astype(BF), h.astype(BF), right.astype(BF)


def put(ref, t, r, h):
    for k, v in enumerate(shifts(h)):
        ref[k, t, r] = v


def pack_weights(weight, packed):
    zero = jnp.zeros((L, L), BF)
    for i in range(3):
        for k in range(3):
            blocks = []
            for j in range(3):
                w = weight[i, j, k * C : (k + 1) * C, :]
                w = jnp.concatenate([w, jnp.zeros((C, L - C), BF)], axis=1)
                blocks.append(jnp.concatenate([w, jnp.zeros((L - C, L), BF)], axis=0))
            for half in range(2):
                for a in range(2):
                    for b in range(2):
                        j = 2 * half + a - b
                        row = (i * 3 + k) * 256 + a * L
                        packed[half, row : row + L, b * L : (b + 1) * L] = blocks[j] if 0 <= j <= 2 else zero


def half_conv(field, frames, row, packed, half):
    pieces = []
    for i in range(3):
        for k in range(3):
            for a in range(2):
                pieces.append(field[k, i : i + frames, row + a].reshape(frames * BW, L))
    return jnp.dot(jnp.concatenate(pieces, axis=1), packed[half], preferred_element_type=F32)


def send_kernel(clip, gain, widths, top, bottom, scratch):
    g = half_gain_of(gain)
    mask = column_mask(widths)
    for t in range(4):
        spread(clip[t].astype(F32), scratch)
        for out, rows in ((top, (0, 1)), (bottom, (6, 7))):
            for n, r in enumerate(rows):
                out[t, n] = settle(scratch[r * BW : (r + 1) * BW, :], g, mask).astype(BF)


def pre_kernel(
    clip, earlier, gain1, weight1, gain2, weight2, widths,
    packed1, packed2, part1, part2, inner, x1, x2, scratch,
):
    mask = column_mask(widths)
    g1, g2 = half_gain_of(gain1), half_gain_of(gain2)
    pack_weights(weight1, packed1)
    pack_weights(weight2, packed2)
    for t in range(8):
        spread((earlier[t] if t < 4 else clip[t - 4]).astype(F32), scratch)
        for r in range(8):
            put(x1, t, r, settle(scratch[r * BW : (r + 1) * BW, :], g1, mask))
    part1[0] = half_conv(x1, 6, 0, packed1, 1)
    part1[1] = half_conv(x1, 6, 6, packed1, 0)
    for p in range(1, 4):
        acc = half_conv(x1, 6, 2 * p - 2, packed1, 0) + half_conv(x1, 6, 2 * p, packed1, 1)
        for t in range(6):
            for b in range(2):
                put(x2, t, 2 * p - 2 + b, settle(acc[t * BW : (t + 1) * BW, b * L : (b + 1) * L], g2, mask))
    part2[0] = half_conv(x2, 4, 0, packed2, 1)
    part2[1] = half_conv(x2, 4, 4, packed2, 0)
    for q in range(1, 3):
        inner[q - 1] = half_conv(x2, 4, 2 * q - 2, packed2, 0) + half_conv(x2, 4, 2 * q, packed2, 1)


def post_kernel(
    clip, up, down, up_early, down_early, gain2, widths, links,
    packed1, packed2, part1, part2, inner, out, x1, x2, scratch,
):
    mask = column_mask(widths)
    g2 = half_gain_of(gain2)
    for side, (now, early) in enumerate(((up, up_early), (down, down_early))):
        link = links[0, side].astype(F32)
        for t in range(8):
            for r in range(2):
                h = (early[t, r] if t < 4 else now[t - 4, r]).astype(F32) * link
                put(x1.at[side], t, r, h)
        acc = part1[side] + half_conv(x1.at[side], 6, 0, packed1, side)
        for t in range(6):
            for b in range(2):
                outer = link if b == side else 1.0
                h = settle(acc[t * BW : (t + 1) * BW, b * L : (b + 1) * L], g2, mask * outer)
                put(x2.at[side], t, b, h)
    outer_rows = [part2[s] + half_conv(x2.at[s], 4, 0, packed2, s) for s in range(2)]
    live = lax.broadcasted_iota(jnp.int32, (8, BW * C), 1) < widths[0] * C
    for t in range(4):
        for q in range(4):
            acc = inner[q - 1] if q in (1, 2) else outer_rows[q // 3]
            for b in range(2):
                r = 2 * q + b
                scratch[r * BW : (r + 1) * BW, :] = acc[t * BW : (t + 1) * BW, b * L : (b + 1) * L]
        pieces = [scratch[pl.ds(w, 8, stride=BW), :][:, :C] for w in range(BW)]
        y = jnp.concatenate(pieces, axis=1)
        out[t] = jnp.where(live, clip[t].astype(F32) + y, 0.0).astype(BF)


def local(clip, gain1, weight1, gain2, weight2, widths, links):
    tiles = lax.axis_size("tile")
    ups = [(i, i + 1) for i in range(tiles - 1)]
    downs = [(i + 1, i) for i in range(tiles - 1)]
    gain1, gain2 = gain1.reshape(1, C), gain2.reshape(1, C)
    edge = VM((4, 2, BW, L), BF)
    top, bottom = pl.pallas_call(
        send_kernel,
        out_shape=(edge, edge),
        in_specs=[vmem, vmem, smem],
        out_specs=(vmem, vmem),
        scratch_shapes=[VM((8 * BW, L), F32)],
        compiler_params=PARAMS,
    )(clip, gain1, widths)
    up = lax.ppermute(bottom, "tile", ups)
    earlier = lax.ppermute(clip, "tm", [(0, 1)])
    down = lax.ppermute(top, "tile", downs)
    packed1, packed2, part1, part2, inner = pl.pallas_call(
        pre_kernel,
        out_shape=(
            VM((2, 9 * 256, 256), BF),
            VM((2, 9 * 256, 256), BF),
            VM((2, 6 * BW, 256), F32),
            VM((2, 4 * BW, 256), F32),
            VM((2, 4 * BW, 256), F32),
        ),
        in_specs=[vmem] * 6 + [smem],
        out_specs=(vmem,) * 5,
        scratch_shapes=[VM((3, 8, 8, BW, L), BF), VM((3, 6, 6, BW, L), BF), VM((8 * BW, L), F32)],
        compiler_params=PARAMS,
    )(clip, earlier, gain1, weight1, gain2, weight2, widths)
    up_early = lax.ppermute(up, "tm", [(0, 1)])
    down_early = lax.ppermute(down, "tm", [(0, 1)])
    return pl.pallas_call(
        post_kernel,
        out_shape=jax.ShapeDtypeStruct((4, 8, BW * C), BF),
        in_specs=[vmem] * 6 + [smem, smem] + [vmem] * 5,
        out_specs=vmem,
        scratch_shapes=[VM((2, 3, 8, 2, BW, L), BF), VM((2, 3, 6, 2, BW, L), BF), VM((8 * BW, L), F32)],
        compiler_params=PARAMS,
    )(clip, up, down, up_early, down_early, gain2, widths, links, packed1, packed2, part1, part2, inner)


def solution(mesh):
    in_specs = (P("tm", "tile", None), P(), P(), P(), P(), P("tile"), P("tile", None))
    out_specs = P("tm", "tile", None)
    return jax.shard_map(local, mesh=mesh, in_specs=in_specs, out_specs=out_specs, check_vma=False)
```

```python
import jax
import jax.numpy as jnp
from jax import lax
from jax.experimental import pallas as pl
from jax.experimental.pallas import tpu as pltpu
from jax.sharding import PartitionSpec as P

C = 96
L = 128
BW = 64
FAR = 32
BF = jnp.bfloat16
F32 = jnp.float32
VM = pltpu.VMEM
vmem = pl.BlockSpec(memory_space=pltpu.VMEM)
smem = pl.BlockSpec(memory_space=pltpu.SMEM)
hbm = pl.BlockSpec(memory_space=pltpu.HBM)
DMA = pltpu.SemaphoreType.DMA
PARAMS = pltpu.CompilerParams(vmem_limit_bytes=32 * 1024 * 1024)


def settle(x, half_gain):
    ms = jnp.sum(x * x, axis=-1, keepdims=True) * (1.0 / C)
    v = x * lax.rsqrt(ms + 1e-6) * half_gain
    return v + v * jnp.tanh(v)


def half_gain_of(gain):
    g = gain[...] * 0.5
    return jnp.concatenate([g, jnp.zeros((1, L - C), F32)], axis=1)


def spread(frame, scratch):
    pad = jnp.zeros((8, L - C), F32)
    for w in range(BW):
        piece = jnp.concatenate([frame[:, w * C : (w + 1) * C], pad], axis=1)
        scratch[pl.ds(w, 8, stride=BW), :] = piece


def shifts(h):
    row = lax.broadcasted_iota(jnp.int32, (BW, 1), 0)
    left = jnp.where(row == 0, 0.0, pltpu.roll(h, 1, 0))
    right = jnp.where(row == BW - 1, 0.0, pltpu.roll(h, BW - 1, 0))
    return left.astype(BF), h.astype(BF), right.astype(BF)


def put(ref, t, r, h):
    for k, v in enumerate(shifts(h)):
        ref[k, t, r] = v


def pack_weights(weight, packed):
    zero = jnp.zeros((L, L), BF)
    for i in range(3):
        for k in range(3):
            blocks = []
            for j in range(3):
                w = weight[i, j, k * C : (k + 1) * C, :]
                w = jnp.concatenate([w, jnp.zeros((C, L - C), BF)], axis=1)
                blocks.append(jnp.concatenate([w, jnp.zeros((L - C, L), BF)], axis=0))
            for half in range(2):
                for a in range(2):
                    for b in range(2):
                        j = 2 * half + a - b
                        row = (i * 3 + k) * 256 + a * L
                        packed[half, row : row + L, b * L : (b + 1) * L] = blocks[j] if 0 <= j <= 2 else zero


def half_conv(field, frames, row, packed, half):
    pieces = []
    for i in range(3):
        for k in range(3):
            for a in range(2):
                pieces.append(field[k, i : i + frames, row + a].reshape(frames * BW, L))
    return jnp.dot(jnp.concatenate(pieces, axis=1), packed[half], preferred_element_type=F32)


def start(*copies):
    copies = [pltpu.make_async_copy(*copy) for copy in copies]
    for copy in copies:
        copy.start()
    return copies


def column_mask(widths):
    return (lax.broadcasted_iota(jnp.int32, (BW, L), 0) < widths[0]).astype(F32)


def masks_of(widths, links):
    mask = column_mask(widths)
    return mask, mask * links[0, 0].astype(F32), mask * links[0, 1].astype(F32)


def is_even():
    return lax.rem(lax.axis_index("tile"), 2) == 0


def is_first():
    return lax.rem(lax.axis_index("tile"), FAR) == 0


def is_last():
    return lax.rem(lax.axis_index("tile"), FAR) == FAR - 1


def send_kernel(
    clip_hbm, gain1_hbm, weight1_hbm, gain2_hbm, weight2_hbm,
    clip, hidden, near, other, other_again, weight1, gain2, weight2, gain1, scratch, sems,
):
    gain_copy = start((gain1_hbm, gain1, sems.at[4]))[0]
    frames = start(*((clip_hbm.at[t], clip.at[t], sems.at[t]) for t in range(4)))
    pairs = ((weight1_hbm, weight1), (gain2_hbm, gain2), (weight2_hbm, weight2))
    rest = start(*((src, dst, sems.at[5 + n]) for n, (src, dst) in enumerate(pairs)))
    gain_copy.wait()
    g = half_gain_of(gain1)
    even = is_even()
    for t in range(4):
        frames[t].wait()
        spread(clip[t].astype(F32), scratch.at[t])
        rows = [settle(scratch[t, r * BW : (r + 1) * BW, :], g) for r in range(8)]
        for r in range(8):
            hidden[t, r] = rows[r].astype(BF)
        for r in range(2):
            near[t, r] = jnp.where(even, rows[6 + r], rows[r]).astype(BF)
            away = jnp.where(even, rows[r], rows[6 + r]).astype(BF)
            other[t, r] = away
            other_again[t, r] = away
    for copy in rest:
        copy.wait()


def pre_body(
    hidden, earlier, weight1, gain2, weight2, widths,
    packed1, packed2, part1, part2, inner, x1, x2,
):
    has_earlier = (lax.axis_index("tm") > 0).astype(F32)
    mask = column_mask(widths)
    early_mask = mask * has_earlier
    g2 = half_gain_of(gain2)
    for t in range(8):
        for r in range(8):
            h = earlier[t, r].astype(F32) * early_mask if t < 4 else hidden[t - 4, r].astype(F32) * mask
            put(x1, t, r, h)
    pack_weights(weight1, packed1)
    pack_weights(weight2, packed2)
    part1[0] = half_conv(x1, 6, 0, packed1, 1)
    part1[1] = half_conv(x1, 6, 6, packed1, 0)
    for p in range(1, 4):
        acc = half_conv(x1, 6, 2 * p - 2, packed1, 0) + half_conv(x1, 6, 2 * p, packed1, 1)
        for t in range(6):
            m = early_mask if t < 2 else mask
            for b in range(2):
                put(x2, t, 2 * p - 2 + b, settle(acc[t * BW : (t + 1) * BW, b * L : (b + 1) * L], g2) * m)
    part2[0] = half_conv(x2, 4, 0, packed2, 1)
    part2[1] = half_conv(x2, 4, 4, packed2, 0)
    for q in range(1, 3):
        inner[q - 1] = half_conv(x2, 4, 2 * q - 2, packed2, 0) + half_conv(x2, 4, 2 * q, packed2, 1)


def pre_first_kernel(*refs):
    @pl.when(is_first())
    def _():
        pre_body(*refs[:6], *refs[8:])


def pre_rest_kernel(*refs):
    @pl.when(jnp.logical_not(is_first()))
    def _():
        pre_body(*refs[:6], *refs[11:])


def halo_kernel(near, other, other_far, halos):
    even = is_even().astype(jnp.int32)
    halos[even] = near[...]

    @pl.when(is_first())
    def _():
        halos[1 - even] = other_far[...]

    @pl.when(jnp.logical_not(is_first()))
    def _():
        halos[1 - even] = other[...]


def post_kernel(
    clip, halos, early_halos, below, early_below, gain2, widths, links, packed1, packed2, part1, part2, inner,
    out_hbm, x1, x2, scratch, out, sems,
):
    g2 = half_gain_of(gain2)
    last = is_last()
    has_earlier = (lax.axis_index("tm") > 0).astype(F32)
    masks = masks_of(widths, links)
    early_masks = [m * has_earlier for m in masks]
    live = lax.broadcasted_iota(jnp.int32, (8, BW * C), 1) < widths[0] * C
    for side in range(2):
        for t in range(8):
            for r in range(2):
                rows, far = (early_halos, early_below) if t < 4 else (halos, below)
                h = rows[side, t % 4, r].astype(F32)
                if side == 1:
                    h = jnp.where(last, far[t % 4, r].astype(F32), h)
                put(x1.at[side], t, r, h * (early_masks if t < 4 else masks)[1 + side])
        acc = part1[side] + half_conv(x1.at[side], 6, 0, packed1, side)
        for t in range(6):
            for b in range(2):
                m = (early_masks if t < 2 else masks)[1 + side if b == side else 0]
                put(x2.at[side], t, b, settle(acc[t * BW : (t + 1) * BW, b * L : (b + 1) * L], g2) * m)
    outer_rows = [part2[s] + half_conv(x2.at[s], 4, 0, packed2, s) for s in range(2)]
    copies = []
    for t in range(4):
        for q in range(4):
            acc = inner[q - 1] if q in (1, 2) else outer_rows[q // 3]
            for b in range(2):
                r = 2 * q + b
                scratch[t, r * BW : (r + 1) * BW, :] = acc[t * BW : (t + 1) * BW, b * L : (b + 1) * L]
        pieces = [scratch[t, pl.ds(w, 8, stride=BW), :][:, :C] for w in range(BW)]
        y = clip[t].astype(F32) + jnp.concatenate(pieces, axis=1)
        out[t] = jnp.where(live, y, 0.0).astype(BF)
        copies += start((out.at[t], out_hbm.at[t], sems.at[t]))
    for copy in copies:
        copy.wait()


def local(clip, gain1, weight1, gain2, weight2, widths, links):
    tiles = lax.axis_size("tile")
    near_pairs = [(i, i ^ 1) for i in range(tiles)]
    last = [i for i in range(FAR - 1, tiles - 1, FAR)]
    ends = {n * FAR + m: (n ^ 1) * FAR + m for n in range(tiles // FAR) for m in (0, FAR - 1)}
    other_pairs = [(i, ends.get(i, ((i + 1) ^ 1) - 1)) for i in range(tiles)]
    cores = [(0, 1), (1, 0)]
    gain1, gain2 = gain1.reshape(1, C), gain2.reshape(1, C)
    clip, gain1, weight1, gain2, weight2 = (
        pltpu.with_memory_space_constraint(x, pltpu.HBM) for x in (clip, gain1, weight1, gain2, weight2)
    )
    edge = VM((4, 2, BW, L), BF)
    weight = VM((3, 3, 3 * C, C), BF)
    clip, hidden, near, other, other_again, weight1, gain2, weight2 = pl.pallas_call(
        send_kernel,
        out_shape=(
            VM((4, 8, BW * C), BF), VM((4, 8, BW, L), BF), edge, edge, edge, weight, VM((1, C), F32), weight,
        ),
        in_specs=[hbm] * 5,
        out_specs=(vmem,) * 8,
        scratch_shapes=[VM((1, C), F32), VM((4, 8 * BW, L), F32), DMA((8,))],
        compiler_params=PARAMS,
    )(clip, gain1, weight1, gain2, weight2)
    from_far = lax.ppermute(other, "tile", [(i, i + 1) for i in last])
    from_near = lax.ppermute(near, "tile", near_pairs)
    from_other = lax.ppermute(other, "tile", other_pairs)
    earlier = lax.ppermute(hidden, "tm", cores)
    state = (
        VM((2, 9 * 256, 256), BF),
        VM((2, 9 * 256, 256), BF),
        VM((2, 6 * BW, 256), F32),
        VM((2, 4 * BW, 256), F32),
        VM((2, 4 * BW, 256), F32),
    )
    inputs = (hidden, earlier, weight1, gain2, weight2, widths)
    specs = [vmem] * 5 + [smem]
    scratch = [
        VM((3, 8, 8, BW, L), BF),
        VM((3, 6, 6, BW, L), BF),
    ]
    first = pl.pallas_call(
        pre_first_kernel,
        out_shape=(edge, *state),
        in_specs=specs + [vmem],
        out_specs=(vmem,) * 6,
        scratch_shapes=scratch,
        input_output_aliases={6: 0},
        compiler_params=PARAMS,
    )(*inputs, other_again)
    below = lax.ppermute(first[0], "tile", [(i + 1, i) for i in last])
    made = pl.pallas_call(
        pre_rest_kernel,
        out_shape=state,
        in_specs=specs + [vmem] * 5,
        out_specs=(vmem,) * 5,
        scratch_shapes=scratch,
        input_output_aliases={6 + n: n for n in range(5)},
        compiler_params=PARAMS,
    )(*inputs, *first[1:])
    from_far, from_near, from_other, made = lax.optimization_barrier((from_far, from_near, from_other, made))
    halos = pl.pallas_call(
        halo_kernel,
        out_shape=VM((2, 4, 2, BW, L), BF),
        in_specs=[vmem] * 3,
        out_specs=vmem,
        compiler_params=PARAMS,
    )(from_near, from_other, from_far)
    below, halos = lax.optimization_barrier((below, halos))
    early_halos = lax.ppermute(halos, "tm", cores)
    early_below = lax.ppermute(below, "tm", cores)
    return pl.pallas_call(
        post_kernel,
        out_shape=pltpu.HBM((4, 8, BW * C), BF),
        in_specs=[vmem] * 6 + [smem, smem] + [vmem] * 5,
        out_specs=hbm,
        scratch_shapes=[
            VM((2, 3, 8, 2, BW, L), BF),
            VM((2, 3, 6, 2, BW, L), BF),
            VM((4, 8 * BW, L), F32),
            VM((4, 8, BW * C), BF),
            DMA((4,)),
        ],
        compiler_params=PARAMS,
    )(clip, halos, early_halos, below, early_below, gain2, widths, links, *made)


def solution(mesh):
    in_specs = (P("tm", "tile", None), P(), P(), P(), P(), P("tile"), P("tile", None))
    out_specs = P("tm", "tile", None)
    return jax.shard_map(local, mesh=mesh, in_specs=in_specs, out_specs=out_specs, check_vma=False)
```

```python
import jax
import jax.numpy as jnp
from jax import lax
from jax.experimental import pallas as pl
from jax.experimental.pallas import tpu as pltpu
from jax.sharding import PartitionSpec as P

C = 96
L = 128
BW = 64
FAR = 32
STEP = BW + 8
BF = jnp.bfloat16
F32 = jnp.float32
VM = pltpu.VMEM
vmem = pl.BlockSpec(memory_space=pltpu.VMEM)
smem = pl.BlockSpec(memory_space=pltpu.SMEM)
hbm = pl.BlockSpec(memory_space=pltpu.HBM)
DMA = pltpu.SemaphoreType.DMA
PARAMS = pltpu.CompilerParams(vmem_limit_bytes=32 * 1024 * 1024)


def settle(x, half_gain):
    ms = jnp.sum(x * x, axis=-1, keepdims=True) * (1.0 / C)
    v = x * lax.rsqrt(ms + 1e-6) * half_gain
    return v + v * jnp.tanh(v)


def half_gain_of(gain):
    g = gain[...] * 0.5
    return jnp.concatenate([g, jnp.zeros((1, L - C), F32)], axis=1)


def spread(frame, scratch):
    pad = jnp.zeros((8, L - C), F32)
    for w in range(BW):
        piece = jnp.concatenate([frame[:, w * C : (w + 1) * C], pad], axis=1)
        scratch[pl.ds(w, 8, stride=STEP), :] = piece


def shifts(h):
    row = lax.broadcasted_iota(jnp.int32, (BW, 1), 0)
    left = jnp.where(row == 0, 0.0, pltpu.roll(h, 1, 0))
    right = jnp.where(row == BW - 1, 0.0, pltpu.roll(h, BW - 1, 0))
    return left.astype(BF), h.astype(BF), right.astype(BF)


def put(ref, t, r, h):
    for k, v in enumerate(shifts(h)):
        ref[k, t, r] = v


def pack_weights(weight, packed):
    zero = jnp.zeros((L, L), BF)
    for i in range(3):
        for k in range(3):
            blocks = []
            for j in range(3):
                w = weight[i, j, k * C : (k + 1) * C, :]
                w = jnp.concatenate([w, jnp.zeros((C, L - C), BF)], axis=1)
                blocks.append(jnp.concatenate([w, jnp.zeros((L - C, L), BF)], axis=0))
            for half in range(2):
                for a in range(2):
                    for b in range(2):
                        j = 2 * half + a - b
                        row = (i * 3 + k) * 256 + a * L
                        packed[half, row : row + L, b * L : (b + 1) * L] = blocks[j] if 0 <= j <= 2 else zero


def half_conv(field, frames, row, packed, half):
    pieces = []
    for i in range(3):
        for k in range(3):
            for a in range(2):
                pieces.append(field[k, i : i + frames, row + a].reshape(frames * BW, L))
    return jnp.dot(jnp.concatenate(pieces, axis=1), packed[half], preferred_element_type=F32)


def start(*copies):
    copies = [pltpu.make_async_copy(*copy) for copy in copies]
    for copy in copies:
        copy.start()
    return copies


def column_mask(widths):
    return (lax.broadcasted_iota(jnp.int32, (BW, L), 0) < widths[0]).astype(F32)


def masks_of(widths, links):
    mask = column_mask(widths)
    return mask, mask * links[0, 0].astype(F32), mask * links[0, 1].astype(F32)


def is_even():
    return lax.rem(lax.axis_index("tile"), 2) == 0


def is_first():
    return lax.rem(lax.axis_index("tile"), FAR) == 0


def is_last():
    return lax.rem(lax.axis_index("tile"), FAR) == FAR - 1


def send_kernel(
    clip_hbm, gain1_hbm, weight1_hbm, gain2_hbm, weight2_hbm,
    clip, hidden, near, other, other_again, weight1, gain2, weight2, gain1, scratch, sems,
):
    gain_copy = start((gain1_hbm, gain1, sems.at[4]))[0]
    frames = start(*((clip_hbm.at[t], clip.at[t], sems.at[t]) for t in range(4)))
    pairs = ((weight1_hbm, weight1), (gain2_hbm, gain2), (weight2_hbm, weight2))
    rest = start(*((src, dst, sems.at[5 + n]) for n, (src, dst) in enumerate(pairs)))
    gain_copy.wait()
    g = half_gain_of(gain1)
    even = is_even()
    for t in range(4):
        frames[t].wait()
        spread(clip[t].astype(F32), scratch.at[t])
        rows = [settle(scratch[t, r * STEP : r * STEP + BW, :], g) for r in range(8)]
        for r in range(8):
            hidden[t, r] = rows[r].astype(BF)
        for r in range(2):
            near[t, r] = jnp.where(even, rows[6 + r], rows[r]).astype(BF)
            away = jnp.where(even, rows[r], rows[6 + r]).astype(BF)
            other[t, r] = away
            other_again[t, r] = away
    for copy in rest:
        copy.wait()


def pre_body(
    hidden, earlier, weight1, gain2, weight2, widths,
    packed1, packed2, part1, part2, inner, x1, x2,
):
    has_earlier = (lax.axis_index("tm") > 0).astype(F32)
    mask = column_mask(widths)
    early_mask = mask * has_earlier
    g2 = half_gain_of(gain2)

    def fill(rows):
        for t in range(8):
            for r in rows:
                h = earlier[t, r].astype(F32) * early_mask if t < 4 else hidden[t - 4, r].astype(F32) * mask
                put(x1, t, r, h)

    def first_pair(p):
        return half_conv(x1, 6, 2 * p - 2, packed1, 0) + half_conv(x1, 6, 2 * p, packed1, 1)

    def settle_pair(p, acc):
        for t in range(6):
            m = early_mask if t < 2 else mask
            for b in range(2):
                put(x2, t, 2 * p - 2 + b, settle(acc[t * BW : (t + 1) * BW, b * L : (b + 1) * L], g2) * m)

    def second_pair(q):
        inner[q - 1] = half_conv(x2, 4, 2 * q - 2, packed2, 0) + half_conv(x2, 4, 2 * q, packed2, 1)

    fill(range(4))
    pack_weights(weight1, packed1)
    acc1 = first_pair(1)
    fill(range(4, 8))
    acc2 = first_pair(2)
    settle_pair(1, acc1)
    acc3 = first_pair(3)
    settle_pair(2, acc2)
    pack_weights(weight2, packed2)
    part1[0] = half_conv(x1, 6, 0, packed1, 1)
    settle_pair(3, acc3)
    second_pair(1)
    part1[1] = half_conv(x1, 6, 6, packed1, 0)
    part2[0] = half_conv(x2, 4, 0, packed2, 1)
    second_pair(2)
    part2[1] = half_conv(x2, 4, 4, packed2, 0)


def pre_first_kernel(*refs):
    @pl.when(is_first())
    def _():
        pre_body(*refs[:6], *refs[8:])


def pre_rest_kernel(*refs):
    @pl.when(jnp.logical_not(is_first()))
    def _():
        pre_body(*refs[:6], *refs[11:])


def halo_kernel(near, other, other_far, above, below):
    @pl.when(is_even())
    def _():
        below[...] = near[...]

        @pl.when(is_first())
        def _():
            above[...] = other_far[...]

        @pl.when(jnp.logical_not(is_first()))
        def _():
            above[...] = other[...]

    @pl.when(jnp.logical_not(is_even()))
    def _():
        above[...] = near[...]
        below[...] = other[...]


def post_kernel(
    clip, above, below, early_above, early_below, far_below, far_early_below, gain2, widths, links, packed1, packed2, part1, part2, inner,
    out_hbm, x1, x2, scratch, out, sems,
):
    g2 = half_gain_of(gain2)
    last = is_last()
    has_earlier = (lax.axis_index("tm") > 0).astype(F32)
    masks = masks_of(widths, links)
    early_masks = [m * has_earlier for m in masks]
    live = lax.broadcasted_iota(jnp.int32, (8, BW * C), 1) < widths[0] * C
    for side in range(2):
        for t in range(8):
            for r in range(2):
                rows = ((early_above, early_below) if t < 4 else (above, below))[side]
                h = rows[t % 4, r].astype(F32)
                if side == 1:
                    far = far_early_below if t < 4 else far_below
                    h = jnp.where(last, far[t % 4, r].astype(F32), h)
                put(x1.at[side], t, r, h * (early_masks if t < 4 else masks)[1 + side])
        acc = part1[side] + half_conv(x1.at[side], 6, 0, packed1, side)
        for t in range(6):
            for b in range(2):
                m = (early_masks if t < 2 else masks)[1 + side if b == side else 0]
                put(x2.at[side], t, b, settle(acc[t * BW : (t + 1) * BW, b * L : (b + 1) * L], g2) * m)
    outer_rows = [part2[s] + half_conv(x2.at[s], 4, 0, packed2, s) for s in range(2)]
    copies = []
    for t in range(4):
        for q in range(4):
            acc = inner[q - 1] if q in (1, 2) else outer_rows[q // 3]
            for b in range(2):
                r = 2 * q + b
                scratch[t, r * STEP : r * STEP + BW, :] = acc[t * BW : (t + 1) * BW, b * L : (b + 1) * L]
        pieces = [scratch[t, pl.ds(w, 8, stride=STEP), :][:, :C] for w in range(BW)]
        y = clip[t].astype(F32) + jnp.concatenate(pieces, axis=1)
        out[t] = jnp.where(live, y, 0.0).astype(BF)
        copies += start((out.at[t], out_hbm.at[t], sems.at[t]))
    for copy in copies:
        copy.wait()


def local(clip, gain1, weight1, gain2, weight2, widths, links):
    tiles = lax.axis_size("tile")
    near_pairs = [(i, i ^ 1) for i in range(tiles)]
    last = [i for i in range(FAR - 1, tiles - 1, FAR)]
    ends = {n * FAR + m: (n ^ 1) * FAR + m for n in range(tiles // FAR) for m in (0, FAR - 1)}
    other_pairs = [(i, ends.get(i, ((i + 1) ^ 1) - 1)) for i in range(tiles)]
    cores = [(0, 1), (1, 0)]
    gain1, gain2 = gain1.reshape(1, C), gain2.reshape(1, C)
    clip, gain1, weight1, gain2, weight2 = (
        pltpu.with_memory_space_constraint(x, pltpu.HBM) for x in (clip, gain1, weight1, gain2, weight2)
    )
    edge = VM((4, 2, BW, L), BF)
    weight = VM((3, 3, 3 * C, C), BF)
    clip, hidden, near, other, other_again, weight1, gain2, weight2 = pl.pallas_call(
        send_kernel,
        out_shape=(
            VM((4, 8, BW * C), BF), VM((4, 8, BW, L), BF), edge, edge, edge, weight, VM((1, C), F32), weight,
        ),
        in_specs=[hbm] * 5,
        out_specs=(vmem,) * 8,
        scratch_shapes=[VM((1, C), F32), VM((4, 8 * STEP, L), F32), DMA((8,))],
        compiler_params=PARAMS,
    )(clip, gain1, weight1, gain2, weight2)
    from_far = lax.ppermute(other, "tile", [(i, i + 1) for i in last])
    from_near = lax.ppermute(near, "tile", near_pairs)
    from_other = lax.ppermute(other, "tile", other_pairs)
    earlier = lax.ppermute(hidden, "tm", cores)
    state = (
        VM((2, 9 * 256, 256), BF),
        VM((2, 9 * 256, 256), BF),
        VM((2, 6 * BW, 256), F32),
        VM((2, 4 * BW, 256), F32),
        VM((2, 4 * BW, 256), F32),
    )
    inputs = (hidden, earlier, weight1, gain2, weight2, widths)
    specs = [vmem] * 5 + [smem]
    scratch = [
        VM((3, 8, 8, BW, L), BF),
        VM((3, 6, 6, BW, L), BF),
    ]
    first = pl.pallas_call(
        pre_first_kernel,
        out_shape=(edge, *state),
        in_specs=specs + [vmem],
        out_specs=(vmem,) * 6,
        scratch_shapes=scratch,
        input_output_aliases={6: 0},
        compiler_params=PARAMS,
    )(*inputs, other_again)
    far_below = lax.ppermute(first[0], "tile", [(i + 1, i) for i in last])
    made = pl.pallas_call(
        pre_rest_kernel,
        out_shape=state,
        in_specs=specs + [vmem] * 5,
        out_specs=(vmem,) * 5,
        scratch_shapes=scratch,
        input_output_aliases={6 + n: n for n in range(5)},
        compiler_params=PARAMS,
    )(*inputs, *first[1:])
    from_far, from_near, from_other, made = lax.optimization_barrier((from_far, from_near, from_other, made))
    above, below = pl.pallas_call(
        halo_kernel,
        out_shape=(edge, edge),
        in_specs=[vmem] * 3,
        out_specs=(vmem, vmem),
        compiler_params=PARAMS,
    )(from_near, from_other, from_far)
    early_above = lax.ppermute(above, "tm", cores)
    early_below = lax.ppermute(below, "tm", cores)
    far_early_below = lax.ppermute(far_below, ("tile", "tm"), [(2 * i, 2 * i + 1) for i in last])
    return pl.pallas_call(
        post_kernel,
        out_shape=pltpu.HBM((4, 8, BW * C), BF),
        in_specs=[vmem] * 8 + [smem, smem] + [vmem] * 5,
        out_specs=hbm,
        scratch_shapes=[
            VM((2, 3, 8, 2, BW, L), BF),
            VM((2, 3, 6, 2, BW, L), BF),
            VM((4, 8 * STEP, L), F32),
            VM((4, 8, BW * C), BF),
            DMA((4,)),
        ],
        compiler_params=PARAMS,
    )(
        clip, above, below, early_above, early_below, far_below, far_early_below, gain2, widths, links, *made
    )


def solution(mesh):
    in_specs = (P("tm", "tile", None), P(), P(), P(), P(), P("tile"), P("tile", None))
    out_specs = P("tm", "tile", None)
    return jax.shard_map(local, mesh=mesh, in_specs=in_specs, out_specs=out_specs, check_vma=False)
```

```python
import jax
import jax.numpy as jnp
from jax import lax
from jax.experimental import pallas as pl
from jax.experimental.pallas import tpu as pltpu
from jax.sharding import PartitionSpec as P

C = 96
L = 128
BW = 64
CORNER = 4
FAR = 32
STEP = BW + 8
BF = jnp.bfloat16
F32 = jnp.float32
VM = pltpu.VMEM
vmem = pl.BlockSpec(memory_space=pltpu.VMEM)
smem = pl.BlockSpec(memory_space=pltpu.SMEM)
hbm = pl.BlockSpec(memory_space=pltpu.HBM)
DMA = pltpu.SemaphoreType.DMA
PARAMS = pltpu.CompilerParams(vmem_limit_bytes=32 * 1024 * 1024)


def settle(x, half_gain):
    ms = jnp.sum(x * x, axis=-1, keepdims=True) * (1.0 / C)
    v = x * lax.rsqrt(ms + 1e-6) * half_gain
    return v + v * jnp.tanh(v)


def half_gain_of(gain):
    g = gain[...] * 0.5
    return jnp.concatenate([g, jnp.zeros((1, L - C), F32)], axis=1)


def spread(frame, scratch):
    pad = jnp.zeros((8, L - C), F32)
    for w in range(BW):
        piece = jnp.concatenate([frame[:, w * C : (w + 1) * C], pad], axis=1)
        scratch[pl.ds(w, 8, stride=STEP), :] = piece


def shifts(h):
    row = lax.broadcasted_iota(jnp.int32, (BW, 1), 0)
    left = jnp.where(row == 0, 0.0, pltpu.roll(h, 1, 0))
    right = jnp.where(row == BW - 1, 0.0, pltpu.roll(h, BW - 1, 0))
    return left.astype(BF), h.astype(BF), right.astype(BF)


def put(ref, t, r, h):
    for k, v in enumerate(shifts(h)):
        ref[k, t, r] = v


def pack_weights(weight, packed):
    zero = jnp.zeros((L, L), BF)
    for i in range(3):
        for k in range(3):
            blocks = []
            for j in range(3):
                w = weight[i, j, k * C : (k + 1) * C, :]
                w = jnp.concatenate([w, jnp.zeros((C, L - C), BF)], axis=1)
                blocks.append(jnp.concatenate([w, jnp.zeros((L - C, L), BF)], axis=0))
            for half in range(2):
                for a in range(2):
                    for b in range(2):
                        j = 2 * half + a - b
                        row = (i * 3 + k) * 256 + a * L
                        packed[half, row : row + L, b * L : (b + 1) * L] = blocks[j] if 0 <= j <= 2 else zero


def half_conv(field, frames, row, packed, half):
    pieces = []
    for i in range(3):
        for k in range(3):
            for a in range(2):
                pieces.append(field[k, i : i + frames, row + a].reshape(frames * BW, L))
    return jnp.dot(jnp.concatenate(pieces, axis=1), packed[half], preferred_element_type=F32)


def start(*copies):
    copies = [pltpu.make_async_copy(*copy) for copy in copies]
    for copy in copies:
        copy.start()
    return copies


def column_mask(widths):
    return (lax.broadcasted_iota(jnp.int32, (BW, L), 0) < widths[0]).astype(F32)


def masks_of(widths, links):
    mask = column_mask(widths)
    return mask, mask * links[0, 0].astype(F32), mask * links[0, 1].astype(F32)


def is_even():
    return lax.rem(lax.axis_index("tile"), 2) == 0


def is_first():
    return lax.rem(lax.axis_index("tile"), FAR) == 0


def send_kernel(
    clip_hbm, gain1_hbm, weight1_hbm, gain2_hbm, weight2_hbm,
    clip, hidden, bottom, near, top, weight1, gain2, weight2, gain1, scratch, sems,
):
    gain_copy = start((gain1_hbm, gain1, sems.at[4]))[0]
    frames = start(*((clip_hbm.at[t], clip.at[t], sems.at[t]) for t in range(4)))
    pairs = ((weight1_hbm, weight1), (gain2_hbm, gain2), (weight2_hbm, weight2))
    rest = start(*((src, dst, sems.at[5 + n]) for n, (src, dst) in enumerate(pairs)))
    gain_copy.wait()
    g = half_gain_of(gain1)
    even = is_even()
    ends = []
    for t in range(4):
        frames[t].wait()
        spread(clip[t].astype(F32), scratch.at[t])
        rows = [settle(scratch[t, r * STEP : r * STEP + BW, :], g) for r in range(8)]
        for r in range(8):
            hidden[t, r] = rows[r].astype(BF)
        ends += [rows]
    for half in range(2):
        first, last = (
            jnp.concatenate([ends[2 * half + t][r + n][:, :C] for t in range(2) for n in range(2)], axis=1)
            for r in (0, 6)
        )
        top[half] = first.astype(BF)
        bottom[half] = last.astype(BF)
        near[half] = jnp.where(even, last, first).astype(BF)
    for copy in rest:
        copy.wait()


def settle_pair(p, acc, g2, masks, x2):
    for t in range(6):
        for b in range(2):
            h = settle(acc[t * BW : (t + 1) * BW, b * L : (b + 1) * L], g2) * masks[t >= 2]
            put(x2, t, 2 * p - 2 + b, h)


def first_pair(p, x1, packed1):
    return half_conv(x1, 6, 2 * p - 2, packed1, 0) + half_conv(x1, 6, 2 * p, packed1, 1)


def both_masks(widths):
    mask = column_mask(widths)
    return mask * (lax.axis_index("tm") > 0).astype(F32), mask


def first_body(hidden, earlier, weight1, gain2, weight2, widths, packed1, packed2, part1, x1, x2):
    masks = both_masks(widths)
    g2 = half_gain_of(gain2)

    def fill(rows):
        for t in range(8):
            for r in rows:
                put(x1, t, r, (earlier if t < 4 else hidden)[t % 4, r].astype(F32) * masks[t >= 4])

    fill(range(4))
    pack_weights(weight1, packed1)
    acc1 = first_pair(1, x1, packed1)
    fill(range(4, 8))
    part1[0] = half_conv(x1, 6, 0, packed1, 1)
    settle_pair(1, acc1, g2, masks, x2)
    pack_weights(weight2, packed2)


def middle_body(gain2, widths, packed1, part1, x1, x2):
    masks = both_masks(widths)
    g2 = half_gain_of(gain2)
    acc2 = first_pair(2, x1, packed1)
    acc3 = first_pair(3, x1, packed1)
    settle_pair(2, acc2, g2, masks, x2)
    part1[1] = half_conv(x1, 6, 6, packed1, 0)
    settle_pair(3, acc3, g2, masks, x2)


def second_body(x2, packed2, part2, inner):
    for q in range(1, 3):
        inner[q - 1] = half_conv(x2, 4, 2 * q - 2, packed2, 0) + half_conv(x2, 4, 2 * q, packed2, 1)
    part2[0] = half_conv(x2, 4, 0, packed2, 1)
    part2[1] = half_conv(x2, 4, 4, packed2, 0)


def is_corner():
    return lax.rem(lax.axis_index("tile"), CORNER) == 0


def early_kernel(*refs):
    packed1, packed2, part1, x1, x2, part2, inner = refs[8:]

    @pl.when(is_corner())
    def _():
        first_body(*refs[:6], packed1, packed2, part1, x1, x2)

    @pl.when(is_first())
    def _():
        middle_body(refs[3], refs[5], packed1, part1, x1, x2)
        second_body(x2, packed2, part2, inner)


def first_kernel(*refs):
    packed1, packed2, part1, x1, x2 = refs[11:]

    @pl.when(jnp.logical_not(is_corner()))
    def _():
        first_body(*refs[:6], packed1, packed2, part1, x1, x2)

    @pl.when(jnp.logical_not(is_first()))
    def _():
        middle_body(refs[3], refs[5], packed1, part1, x1, x2)


def second_kernel(x2, packed2, part2_in, inner_in, part2, inner):
    @pl.when(jnp.logical_not(is_first()))
    def _():
        second_body(x2, packed2, part2, inner)


def post_kernel(
    clip, above, early_above, near, early_near, other, early_other, gain2, widths, links, packed1, packed2, part1, part2, inner,
    out_hbm, x1, x2, scratch, out, sems,
):
    g2 = half_gain_of(gain2)
    even = is_even()
    has_earlier = (lax.axis_index("tm") > 0).astype(F32)
    masks = masks_of(widths, links)
    early_masks = [m * has_earlier for m in masks]
    live = lax.broadcasted_iota(jnp.int32, (8, BW * C), 1) < widths[0] * C
    pad = jnp.zeros((BW, L - C), F32)
    for side in range(2):
        for half in range(4):
            pick = ((early_above, early_near, early_other), (above, near, other))[half // 2][side : side + 2]
            wide = jnp.where(even, *(rows[half % 2].astype(F32) for rows in pick))
            for n in range(4):
                h = jnp.concatenate([wide[:, n * C : (n + 1) * C], pad], axis=1)
                put(x1.at[side], 2 * half + n // 2, n % 2, h * (early_masks if half < 2 else masks)[1 + side])
        acc = part1[side] + half_conv(x1.at[side], 6, 0, packed1, side)
        for t in range(6):
            for b in range(2):
                m = (early_masks if t < 2 else masks)[1 + side if b == side else 0]
                put(x2.at[side], t, b, settle(acc[t * BW : (t + 1) * BW, b * L : (b + 1) * L], g2) * m)
    outer_rows = [part2[s] + half_conv(x2.at[s], 4, 0, packed2, s) for s in range(2)]
    copies = []
    for t in range(4):
        for q in range(4):
            acc = inner[q - 1] if q in (1, 2) else outer_rows[q // 3]
            for b in range(2):
                r = 2 * q + b
                scratch[t, r * STEP : r * STEP + BW, :] = acc[t * BW : (t + 1) * BW, b * L : (b + 1) * L]
        pieces = [scratch[t, pl.ds(w, 8, stride=STEP), :][:, :C] for w in range(BW)]
        y = clip[t].astype(F32) + jnp.concatenate(pieces, axis=1)
        out[t] = jnp.where(live, y, 0.0).astype(BF)
        copies += start((out.at[t], out_hbm.at[t], sems.at[t]))
    for copy in copies:
        copy.wait()


def local(clip, gain1, weight1, gain2, weight2, widths, links):
    tiles = lax.axis_size("tile")
    near_pairs = [(i, i ^ 1) for i in range(tiles)]
    odd_pairs = [(i + 1, i) for i in range(1, tiles - 1, 2)]
    cores = [(0, 1), (1, 0)]
    gain1, gain2 = gain1.reshape(1, C), gain2.reshape(1, C)
    clip, gain1, weight1, gain2, weight2 = (
        pltpu.with_memory_space_constraint(x, pltpu.HBM) for x in (clip, gain1, weight1, gain2, weight2)
    )
    edge = VM((2, BW, 4 * C), BF)
    weight = VM((3, 3, 3 * C, C), BF)
    clip, hidden, bottom, near, top, weight1, gain2, weight2 = pl.pallas_call(
        send_kernel,
        out_shape=(
            VM((4, 8, BW * C), BF), VM((4, 8, BW, L), BF), edge, edge, edge, weight, VM((1, C), F32), weight,
        ),
        in_specs=[hbm] * 5,
        out_specs=(vmem,) * 8,
        scratch_shapes=[VM((1, C), F32), VM((4, 8 * STEP, L), F32), DMA((8,))],
        compiler_params=PARAMS,
    )(clip, gain1, weight1, gain2, weight2)
    turn = tiles - FAR // 2
    ups = {i: i + 1 for i in range(tiles)} | {turn: 0, tiles - 1: turn + 1}
    above = lax.ppermute(bottom, "tile", list(ups.items()))
    near = lax.ppermute(near, "tile", near_pairs)
    earlier = lax.ppermute(hidden, "tm", cores)
    state = (
        VM((2, 9 * 256, 256), BF),
        VM((2, 9 * 256, 256), BF),
        VM((2, 6 * BW, 256), F32),
        VM((3, 8, 8, BW, L), BF),
        VM((3, 6, 6, BW, L), BF),
        VM((2, 4 * BW, 256), F32),
        VM((2, 4 * BW, 256), F32),
    )
    inputs = (hidden, earlier, weight1, gain2, weight2, widths)
    specs = [vmem] * 5 + [smem]
    top, *made = pl.pallas_call(
        early_kernel,
        out_shape=(edge, *state),
        in_specs=specs + [vmem],
        out_specs=(vmem,) * 8,
        input_output_aliases={6: 0},
        compiler_params=PARAMS,
    )(*inputs, top)
    other = lax.ppermute(top, "tile", odd_pairs)
    packed1, packed2, part1, _, x2 = pl.pallas_call(
        first_kernel,
        out_shape=state[:5],
        in_specs=specs + [vmem] * 5,
        out_specs=(vmem,) * 5,
        input_output_aliases={6 + n: n for n in range(5)},
        compiler_params=PARAMS,
    )(*inputs, *made[:5])
    above, near, x2 = lax.optimization_barrier((above, near, x2))
    early_above = lax.ppermute(above, "tm", cores)
    early_near = lax.ppermute(near, "tm", cores)
    part2, inner = pl.pallas_call(
        second_kernel,
        out_shape=state[5:],
        in_specs=[vmem] * 4,
        out_specs=(vmem,) * 2,
        input_output_aliases={2: 0, 3: 1},
        compiler_params=PARAMS,
    )(x2, packed2, *made[5:])
    other, part2 = lax.optimization_barrier((other, part2))
    early_other = lax.ppermute(other, ("tile", "tm"), [(2 * i, 2 * i + 1) for i in range(1, tiles, 2)])
    return pl.pallas_call(
        post_kernel,
        out_shape=pltpu.HBM((4, 8, BW * C), BF),
        in_specs=[vmem] * 8 + [smem, smem] + [vmem] * 5,
        out_specs=hbm,
        scratch_shapes=[
            VM((2, 3, 8, 2, BW, L), BF),
            VM((2, 3, 6, 2, BW, L), BF),
            VM((4, 8 * STEP, L), F32),
            VM((4, 8, BW * C), BF),
            DMA((4,)),
        ],
        compiler_params=PARAMS,
    )(
        clip, above, early_above, near, early_near, other, early_other, gain2, widths, links,
        packed1, packed2, part1, part2, inner,
    )


def solution(mesh):
    in_specs = (P("tm", "tile", None), P(), P(), P(), P(), P("tile"), P("tile", None))
    out_specs = P("tm", "tile", None)
    return jax.shard_map(local, mesh=mesh, in_specs=in_specs, out_specs=out_specs, check_vma=False)
```

```python
import jax
import jax.numpy as jnp
from jax import lax
from jax.experimental import pallas as pl
from jax.experimental.pallas import tpu as pltpu
from jax.sharding import PartitionSpec as P

C = 96
L = 128
BW = 64
CORNER = 4
FAR = 32
STEP = BW + 8
BF = jnp.bfloat16
F32 = jnp.float32
VM = pltpu.VMEM
vmem = pl.BlockSpec(memory_space=pltpu.VMEM)
smem = pl.BlockSpec(memory_space=pltpu.SMEM)
hbm = pl.BlockSpec(memory_space=pltpu.HBM)
DMA = pltpu.SemaphoreType.DMA
SMALL = pl.CostEstimate(flops=1, bytes_accessed=1, transcendentals=0)
LARGE = pl.CostEstimate(flops=10**10, bytes_accessed=10**7, transcendentals=10**6)
PARAMS = pltpu.CompilerParams(vmem_limit_bytes=32 * 1024 * 1024)


def settle(x, half_gain):
    ms = jnp.sum(x * x, axis=-1, keepdims=True) * (1.0 / C)
    v = x * lax.rsqrt(ms + 1e-6) * half_gain
    return v + v * jnp.tanh(v)


def half_gain_of(gain):
    g = gain[...] * 0.5
    return jnp.concatenate([g, jnp.zeros((1, L - C), F32)], axis=1)


def spread(frame, scratch):
    pad = jnp.zeros((8, L - C), F32)
    for w in range(BW):
        piece = jnp.concatenate([frame[:, w * C : (w + 1) * C], pad], axis=1)
        scratch[pl.ds(w, 8, stride=STEP), :] = piece


def shifts(h):
    row = lax.broadcasted_iota(jnp.int32, (BW, 1), 0)
    left = jnp.where(row == 0, 0.0, pltpu.roll(h, 1, 0))
    right = jnp.where(row == BW - 1, 0.0, pltpu.roll(h, BW - 1, 0))
    return left.astype(BF), h.astype(BF), right.astype(BF)


def put(ref, t, r, h):
    for k, v in enumerate(shifts(h)):
        ref[k, t, r] = v


def pack_weights(weight, packed):
    zero = jnp.zeros((L, L), BF)
    for i in range(3):
        for k in range(3):
            blocks = []
            for j in range(3):
                w = weight[i, j, k * C : (k + 1) * C, :]
                w = jnp.concatenate([w, jnp.zeros((C, L - C), BF)], axis=1)
                blocks.append(jnp.concatenate([w, jnp.zeros((L - C, L), BF)], axis=0))
            for half in range(2):
                for a in range(2):
                    for b in range(2):
                        j = 2 * half + a - b
                        row = (i * 3 + k) * 256 + a * L
                        packed[half, row : row + L, b * L : (b + 1) * L] = blocks[j] if 0 <= j <= 2 else zero


def half_conv(field, frames, row, packed, half):
    pieces = []
    for i in range(3):
        for k in range(3):
            for a in range(2):
                pieces.append(field[k, i : i + frames, row + a].reshape(frames * BW, L))
    return jnp.dot(jnp.concatenate(pieces, axis=1), packed[half], preferred_element_type=F32)


def start(*copies):
    copies = [pltpu.make_async_copy(*copy) for copy in copies]
    for copy in copies:
        copy.start()
    return copies


def column_mask(widths):
    return (lax.broadcasted_iota(jnp.int32, (BW, L), 0) < widths[0]).astype(F32)


def masks_of(widths, links):
    mask = column_mask(widths)
    return mask, mask * links[:, 0:1].astype(F32), mask * links[:, 1:2].astype(F32)


def is_even():
    return lax.rem(lax.axis_index("tile"), 2) == 0


def is_first():
    return lax.rem(lax.axis_index("tile"), FAR) == 0


def send_kernel(
    clip_hbm, gain1_hbm, weight1_hbm, gain2_hbm, weight2_hbm,
    clip, hidden, bottom, near, top, weight1, gain2, weight2, gain1, scratch, sems,
):
    gain_copy = start((gain1_hbm, gain1, sems.at[4]))[0]
    frames = start(*((clip_hbm.at[t], clip.at[t], sems.at[t]) for t in range(4)))
    pairs = ((weight1_hbm, weight1), (gain2_hbm, gain2), (weight2_hbm, weight2))
    rest = start(*((src, dst, sems.at[5 + n]) for n, (src, dst) in enumerate(pairs)))
    gain_copy.wait()
    g = half_gain_of(gain1)
    even = is_even()
    ends = []
    for t in range(4):
        frames[t].wait()
        spread(clip[t].astype(F32), scratch.at[t])
        rows = [settle(scratch[t, r * STEP : r * STEP + BW, :], g) for r in range(8)]
        for r in range(8):
            hidden[t, r] = rows[r].astype(BF)
        ends += [rows]
    for half in range(2):
        first, last = (
            jnp.concatenate([ends[2 * half + t][r + n][:, :C] for t in range(2) for n in range(2)], axis=1)
            for r in (0, 6)
        )
        top[half] = first.astype(BF)
        bottom[half] = last.astype(BF)
        near[half] = jnp.where(even, last, first).astype(BF)
    for copy in rest:
        copy.wait()


def settle_pair(p, acc, g2, masks, x2):
    for t in range(6):
        for b in range(2):
            h = settle(acc[t * BW : (t + 1) * BW, b * L : (b + 1) * L], g2) * masks[t >= 2]
            put(x2, t, 2 * p - 2 + b, h)


def first_pair(p, x1, packed1):
    return half_conv(x1, 6, 2 * p - 2, packed1, 0) + half_conv(x1, 6, 2 * p, packed1, 1)


def both_masks(widths):
    mask = column_mask(widths)
    return mask * (lax.axis_index("tm") > 0).astype(F32), mask


def first_body(hidden, earlier, weight1, gain2, weight2, widths, packed1, packed2, part1, x1, x2):
    masks = both_masks(widths)
    g2 = half_gain_of(gain2)

    def fill(rows):
        for t in range(8):
            for r in rows:
                put(x1, t, r, (earlier if t < 4 else hidden)[t % 4, r].astype(F32) * masks[t >= 4])

    fill(range(4))
    pack_weights(weight1, packed1)
    acc1 = first_pair(1, x1, packed1)
    fill(range(4, 8))
    part1[0] = half_conv(x1, 6, 0, packed1, 1)
    settle_pair(1, acc1, g2, masks, x2)
    pack_weights(weight2, packed2)


def middle_body(gain2, widths, packed1, part1, x1, x2):
    masks = both_masks(widths)
    g2 = half_gain_of(gain2)
    acc2 = first_pair(2, x1, packed1)
    acc3 = first_pair(3, x1, packed1)
    settle_pair(2, acc2, g2, masks, x2)
    part1[1] = half_conv(x1, 6, 6, packed1, 0)
    settle_pair(3, acc3, g2, masks, x2)


def second_body(x2, packed2, part2, inner):
    for q in range(1, 3):
        inner[q - 1] = half_conv(x2, 4, 2 * q - 2, packed2, 0) + half_conv(x2, 4, 2 * q, packed2, 1)
    part2[0] = half_conv(x2, 4, 0, packed2, 1)
    part2[1] = half_conv(x2, 4, 4, packed2, 0)


def is_corner():
    return lax.rem(lax.axis_index("tile"), CORNER) == 0


def early_kernel(*refs):
    packed1, packed2, part1, x1, x2, part2, inner = refs[8:]

    @pl.when(is_corner())
    def _():
        first_body(*refs[:6], packed1, packed2, part1, x1, x2)

    @pl.when(is_first())
    def _():
        middle_body(refs[3], refs[5], packed1, part1, x1, x2)
        second_body(x2, packed2, part2, inner)


def first_kernel(*refs):
    packed1, packed2, part1, x1, x2 = refs[11:]

    @pl.when(jnp.logical_not(is_corner()))
    def _():
        first_body(*refs[:6], packed1, packed2, part1, x1, x2)

    @pl.when(jnp.logical_not(is_first()))
    def _():
        middle_body(refs[3], refs[5], packed1, part1, x1, x2)


def second_kernel(x2, packed2, part2_in, inner_in, part2, inner):
    @pl.when(jnp.logical_not(is_first()))
    def _():
        second_body(x2, packed2, part2, inner)


def post_body(
    ends, clip, gain2, widths, links, packed1, packed2, part1, part2, inner, out_hbm, x1, x2, scratch, out, sems
):
    g2 = half_gain_of(gain2)
    masks = masks_of(widths, links)
    has_earlier = (lax.axis_index("tm") > 0).astype(F32)
    early_masks = [m * has_earlier for m in masks]
    live = lax.broadcasted_iota(jnp.int32, (8, BW * C), 1) < widths[0] * C
    pad = jnp.zeros((BW, L - C), F32)
    for side in range(2):
        for half in range(4):
            wide = ends[side][half // 2][half % 2][...].astype(F32)
            for n in range(4):
                h = jnp.concatenate([wide[:, n * C : (n + 1) * C], pad], axis=1)
                put(x1.at[side], 2 * half + n // 2, n % 2, h * (early_masks if half < 2 else masks)[1 + side])
        acc = part1[side] + half_conv(x1.at[side], 6, 0, packed1, side)
        for t in range(6):
            for b in range(2):
                m = (early_masks if t < 2 else masks)[1 + side if b == side else 0]
                put(x2.at[side], t, b, settle(acc[t * BW : (t + 1) * BW, b * L : (b + 1) * L], g2) * m)
    outer = [part2[s] + half_conv(x2.at[s], 4, 0, packed2, s) for s in range(2)]
    copies = []
    for t in range(4):
        for q, acc in enumerate((outer[0], inner.at[0], inner.at[1], outer[1])):
            for b in range(2):
                r = 2 * q + b
                scratch[t, r * STEP : r * STEP + BW, :] = acc[t * BW : (t + 1) * BW, b * L : (b + 1) * L]
        pieces = [scratch[t, pl.ds(w, 8, stride=STEP), :][:, :C] for w in range(BW)]
        y = clip[t].astype(F32) + jnp.concatenate(pieces, axis=1)
        out[t] = jnp.where(live, y, 0.0).astype(BF)
        copies += start((out.at[t], out_hbm.at[t], sems.at[t]))
    for copy in copies:
        copy.wait()


def split_kernel(above, near, *halves):
    for n in range(2):
        halves[n][...] = above[n]
        halves[2 + n][...] = near[n]


def even_kernel(*refs):
    @pl.when(is_even())
    def _():
        post_body(((refs[:2], refs[2:4]), (refs[4:6], refs[6:8])), *refs[8:])


def odd_kernel(*refs):
    @pl.when(jnp.logical_not(is_even()))
    def _():
        post_body(((refs[:2], refs[2:4]), refs[4:6]), *refs[7:])


def local(clip, gain1, weight1, gain2, weight2, widths, links):
    tiles = lax.axis_size("tile")
    near_pairs = [(i, i ^ 1) for i in range(tiles)]
    odd_pairs = [(i + 1, i) for i in range(1, tiles - 1, 2)]
    cores = [(0, 1), (1, 0)]
    gain1, gain2 = gain1.reshape(1, C), gain2.reshape(1, C)
    clip, gain1, weight1, gain2, weight2 = (
        pltpu.with_memory_space_constraint(x, pltpu.HBM) for x in (clip, gain1, weight1, gain2, weight2)
    )
    edge = VM((2, BW, 4 * C), BF)
    weight = VM((3, 3, 3 * C, C), BF)
    clip, hidden, bottom, near, top, weight1, gain2, weight2 = pl.pallas_call(
        send_kernel,
        out_shape=(
            VM((4, 8, BW * C), BF), VM((4, 8, BW, L), BF), edge, edge, edge, weight, VM((1, C), F32), weight,
        ),
        in_specs=[hbm] * 5,
        out_specs=(vmem,) * 8,
        scratch_shapes=[VM((1, C), F32), VM((4, 8 * STEP, L), F32), DMA((8,))],
        compiler_params=PARAMS,
    )(clip, gain1, weight1, gain2, weight2)
    turn = tiles - FAR // 2
    ups = {i: i + 1 for i in range(tiles)} | {turn: 0, tiles - 1: turn + 1}
    above = lax.ppermute(bottom, "tile", list(ups.items()))
    near = lax.ppermute(near, "tile", near_pairs)
    earlier = lax.ppermute(hidden, "tm", cores)
    state = (
        VM((2, 9 * 256, 256), BF),
        VM((2, 9 * 256, 256), BF),
        VM((2, 6 * BW, 256), F32),
        VM((3, 8, 8, BW, L), BF),
        VM((3, 6, 6, BW, L), BF),
        VM((2, 4 * BW, 256), F32),
        VM((2, 4 * BW, 256), F32),
    )
    inputs = (hidden, earlier, weight1, gain2, weight2, widths)
    specs = [vmem] * 5 + [smem]
    top, *made = pl.pallas_call(
        early_kernel,
        out_shape=(edge, *state),
        in_specs=specs + [vmem],
        out_specs=(vmem,) * 8,
        input_output_aliases={6: 0},
        compiler_params=PARAMS,
    )(*inputs, top)
    other = lax.ppermute(top, "tile", odd_pairs)
    packed1, packed2, part1, _, x2 = pl.pallas_call(
        first_kernel,
        out_shape=state[:5],
        in_specs=specs + [vmem] * 5,
        out_specs=(vmem,) * 5,
        input_output_aliases={6 + n: n for n in range(5)},
        compiler_params=PARAMS,
    )(*inputs, *made[:5])
    above, near, x2 = lax.optimization_barrier((above, near, x2))
    half = VM((BW, 4 * C), BF)
    halves = pl.pallas_call(
        split_kernel,
        out_shape=(half,) * 4,
        in_specs=[vmem] * 2,
        out_specs=(vmem,) * 4,
        cost_estimate=SMALL,
        compiler_params=PARAMS,
    )(above, near)
    early_halves = [lax.ppermute(x, "tm", cores) for x in halves]
    above = (*early_halves[:2], *halves[:2])
    near = (*early_halves[2:], *halves[2:])
    part2, inner = pl.pallas_call(
        second_kernel,
        out_shape=state[5:],
        in_specs=[vmem] * 4,
        out_specs=(vmem,) * 2,
        input_output_aliases={2: 0, 3: 1},
        cost_estimate=SMALL,
        compiler_params=PARAMS,
    )(x2, packed2, *made[5:])
    early_other = lax.ppermute(other, "tm", cores)
    inputs = (clip, gain2, widths, links, packed1, packed2, part1, part2, inner)
    specs = [vmem] * 2 + [smem] + [vmem] * 6
    out = pltpu.HBM((4, 8, BW * C), BF)
    scratch = [
        VM((2, 3, 8, 2, BW, L), BF),
        VM((2, 3, 6, 2, BW, L), BF),
        VM((4, 8 * STEP, L), F32),
        VM((4, 8, BW * C), BF),
        DMA((4,)),
    ]
    done = pl.pallas_call(
        even_kernel,
        out_shape=out,
        in_specs=[vmem] * 8 + specs,
        out_specs=hbm,
        scratch_shapes=scratch,
        cost_estimate=LARGE,
        compiler_params=PARAMS,
    )(*above, *near, *inputs)
    return pl.pallas_call(
        odd_kernel,
        out_shape=out,
        in_specs=[vmem] * 6 + [hbm] + specs,
        out_specs=hbm,
        scratch_shapes=scratch,
        input_output_aliases={6: 0},
        compiler_params=PARAMS,
    )(*near, early_other, other, done, *inputs)


def solution(mesh):
    in_specs = (P("tm", "tile", None), P(), P(), P(), P(), P("tile"), P("tile", None))
    out_specs = P("tm", "tile", None)
    return jax.shard_map(local, mesh=mesh, in_specs=in_specs, out_specs=out_specs, check_vma=False)
```

```python
import jax
import jax.numpy as jnp
from jax import lax
from jax.experimental import pallas as pl
from jax.experimental.pallas import tpu as pltpu
from jax.sharding import PartitionSpec as P

C = 96
L = 128
BW = 64
CORNER = 4
FAR = 32
STEP = BW + 8
BF = jnp.bfloat16
F32 = jnp.float32
VM = pltpu.VMEM
vmem = pl.BlockSpec(memory_space=pltpu.VMEM)
smem = pl.BlockSpec(memory_space=pltpu.SMEM)
hbm = pl.BlockSpec(memory_space=pltpu.HBM)
DMA = pltpu.SemaphoreType.DMA
SMALL = pl.CostEstimate(flops=1, bytes_accessed=1, transcendentals=0)
LARGE = pl.CostEstimate(flops=10**10, bytes_accessed=10**7, transcendentals=10**6)
PARAMS = pltpu.CompilerParams(vmem_limit_bytes=32 * 1024 * 1024)


def settle(x, half_gain):
    ms = jnp.sum(x * x, axis=-1, keepdims=True) * (1.0 / C)
    v = x * lax.rsqrt(ms + 1e-6) * half_gain
    return v + v * jnp.tanh(v)


def half_gain_of(gain):
    g = gain[...] * 0.5
    return jnp.concatenate([g, jnp.zeros((1, L - C), F32)], axis=1)


def spread(frame, scratch):
    pad = jnp.zeros((8, L - C), F32)
    for w in range(BW):
        piece = jnp.concatenate([frame[:, w * C : (w + 1) * C], pad], axis=1)
        scratch[pl.ds(w, 8, stride=STEP), :] = piece


def shifts(h):
    row = lax.broadcasted_iota(jnp.int32, (BW, 1), 0)
    left = jnp.where(row == 0, 0.0, pltpu.roll(h, 1, 0))
    right = jnp.where(row == BW - 1, 0.0, pltpu.roll(h, BW - 1, 0))
    return left.astype(BF), h.astype(BF), right.astype(BF)


def put(ref, t, r, h):
    for k, v in enumerate(shifts(h)):
        ref[k, t, r] = v


def pack_weights(weight, packed):
    zero = jnp.zeros((L, L), BF)
    for i in range(3):
        for k in range(3):
            blocks = []
            for j in range(3):
                w = weight[i, j, k * C : (k + 1) * C, :]
                w = jnp.concatenate([w, jnp.zeros((C, L - C), BF)], axis=1)
                blocks.append(jnp.concatenate([w, jnp.zeros((L - C, L), BF)], axis=0))
            for half in range(2):
                for a in range(2):
                    for b in range(2):
                        j = 2 * half + a - b
                        row = (i * 3 + k) * 256 + a * L
                        packed[half, row : row + L, b * L : (b + 1) * L] = blocks[j] if 0 <= j <= 2 else zero


def half_conv(field, frames, row, packed, half):
    pieces = []
    for i in range(3):
        for k in range(3):
            for a in range(2):
                pieces.append(field[k, i : i + frames, row + a].reshape(frames * BW, L))
    return jnp.dot(jnp.concatenate(pieces, axis=1), packed[half], preferred_element_type=F32)


def start(*copies):
    copies = [pltpu.make_async_copy(*copy) for copy in copies]
    for copy in copies:
        copy.start()
    return copies


def column_mask(widths):
    return (lax.broadcasted_iota(jnp.int32, (BW, L), 0) < widths[0]).astype(F32)


def masks_of(widths, links):
    mask = column_mask(widths)
    return mask, mask * links[:, 0:1].astype(F32), mask * links[:, 1:2].astype(F32)


def is_even():
    return lax.rem(lax.axis_index("tile"), 2) == 0


def is_first():
    return lax.rem(lax.axis_index("tile"), FAR) == 0


def send_kernel(
    clip_hbm, gain1_hbm, weight1_hbm, gain2_hbm, weight2_hbm,
    clip, hidden, bottom, near, top, weight1, gain2, weight2, gain1, scratch, sems,
):
    gain_copy = start((gain1_hbm, gain1, sems.at[4]))[0]
    frames = start(*((clip_hbm.at[t], clip.at[t], sems.at[t]) for t in range(4)))
    pairs = ((weight1_hbm, weight1), (gain2_hbm, gain2), (weight2_hbm, weight2))
    rest = start(*((src, dst, sems.at[5 + n]) for n, (src, dst) in enumerate(pairs)))
    gain_copy.wait()
    g = half_gain_of(gain1)
    even = is_even()
    ends = []
    for t in range(4):
        frames[t].wait()
        spread(clip[t].astype(F32), scratch.at[t])
        rows = [settle(scratch[t, r * STEP : r * STEP + BW, :], g) for r in range(8)]
        for r in range(8):
            hidden[t, r] = rows[r].astype(BF)
        ends += [rows]
    for half in range(2):
        first, last = (
            jnp.concatenate([ends[2 * half + t][r + n][:, :C] for t in range(2) for n in range(2)], axis=1)
            for r in (0, 6)
        )
        top[half] = first.astype(BF)
        bottom[half] = last.astype(BF)
        near[half] = jnp.where(even, last, first).astype(BF)
    for copy in rest:
        copy.wait()


def settle_pair(p, acc, g2, masks, x2):
    for t in range(6):
        for b in range(2):
            h = settle(acc[t * BW : (t + 1) * BW, b * L : (b + 1) * L], g2) * masks[t >= 2]
            put(x2, t, 2 * p - 2 + b, h)


def first_pair(p, x1, packed1):
    return half_conv(x1, 6, 2 * p - 2, packed1, 0) + half_conv(x1, 6, 2 * p, packed1, 1)


def both_masks(widths):
    mask = column_mask(widths)
    return mask * (lax.axis_index("tm") > 0).astype(F32), mask


def first_body(hidden, earlier, weight1, gain2, weight2, widths, packed1, packed2, part1, x1, x2):
    masks = both_masks(widths)
    g2 = half_gain_of(gain2)

    def fill(rows):
        for t in range(8):
            for r in rows:
                put(x1, t, r, (earlier if t < 4 else hidden)[t % 4, r].astype(F32) * masks[t >= 4])

    fill(range(4))
    pack_weights(weight1, packed1)
    acc1 = first_pair(1, x1, packed1)
    fill(range(4, 8))
    part1[0] = half_conv(x1, 6, 0, packed1, 1)
    settle_pair(1, acc1, g2, masks, x2)
    pack_weights(weight2, packed2)


def middle_body(gain2, widths, packed1, part1, x1, x2):
    masks = both_masks(widths)
    g2 = half_gain_of(gain2)
    acc2 = first_pair(2, x1, packed1)
    acc3 = first_pair(3, x1, packed1)
    settle_pair(2, acc2, g2, masks, x2)
    part1[1] = half_conv(x1, 6, 6, packed1, 0)
    settle_pair(3, acc3, g2, masks, x2)


def second_body(x2, packed2, part2, inner):
    for q in range(1, 3):
        inner[q - 1] = half_conv(x2, 4, 2 * q - 2, packed2, 0) + half_conv(x2, 4, 2 * q, packed2, 1)
    part2[0] = half_conv(x2, 4, 0, packed2, 1)
    part2[1] = half_conv(x2, 4, 4, packed2, 0)


def is_corner():
    return lax.rem(lax.axis_index("tile"), CORNER) == 0


def early_kernel(*refs):
    packed1, packed2, part1, x1, x2, part2, inner = refs[8:]

    @pl.when(jnp.logical_and(is_corner(), jnp.logical_not(is_first())))
    def _():
        first_body(*refs[:6], packed1, packed2, part1, x1, x2)

    @pl.when(is_first())
    def _():
        first_body(*refs[:6], packed1, packed2, part1, x1, x2)
        middle_body(refs[3], refs[5], packed1, part1, x1, x2)
        second_body(x2, packed2, part2, inner)


def first_kernel(*refs):
    packed1, packed2, part1, x1, x2 = refs[11:]

    @pl.when(jnp.logical_not(is_corner()))
    def _():
        first_body(*refs[:6], packed1, packed2, part1, x1, x2)

    @pl.when(jnp.logical_not(is_first()))
    def _():
        middle_body(refs[3], refs[5], packed1, part1, x1, x2)


def second_kernel(x2, packed2, part2_in, inner_in, part2, inner):
    @pl.when(jnp.logical_not(is_first()))
    def _():
        second_body(x2, packed2, part2, inner)


def post_body(
    ends, clip, gain2, widths, links, packed1, packed2, part1, part2, inner, out_hbm, x1, x2, scratch, out, sems
):
    g2 = half_gain_of(gain2)
    masks = masks_of(widths, links)
    has_earlier = (lax.axis_index("tm") > 0).astype(F32)
    early_masks = [m * has_earlier for m in masks]
    live = lax.broadcasted_iota(jnp.int32, (8, BW * C), 1) < widths[0] * C
    pad = jnp.zeros((BW, L - C), F32)
    for side in range(2):
        for half in range(4):
            wide = ends[side][half // 2][half % 2][...].astype(F32)
            for n in range(4):
                h = jnp.concatenate([wide[:, n * C : (n + 1) * C], pad], axis=1)
                put(x1.at[side], 2 * half + n // 2, n % 2, h * (early_masks if half < 2 else masks)[1 + side])
        acc = part1[side] + half_conv(x1.at[side], 6, 0, packed1, side)
        for t in range(6):
            for b in range(2):
                m = (early_masks if t < 2 else masks)[1 + side if b == side else 0]
                put(x2.at[side], t, b, settle(acc[t * BW : (t + 1) * BW, b * L : (b + 1) * L], g2) * m)
    outer = [part2[s] + half_conv(x2.at[s], 4, 0, packed2, s) for s in range(2)]
    copies = []
    for t in range(4):
        for q, acc in enumerate((outer[0], inner.at[0], inner.at[1], outer[1])):
            for b in range(2):
                r = 2 * q + b
                scratch[t, r * STEP : r * STEP + BW, :] = acc[t * BW : (t + 1) * BW, b * L : (b + 1) * L]
        pieces = [scratch[t, pl.ds(w, 8, stride=STEP), :][:, :C] for w in range(BW)]
        y = clip[t].astype(F32) + jnp.concatenate(pieces, axis=1)
        out[t] = jnp.where(live, y, 0.0).astype(BF)
        copies += start((out.at[t], out_hbm.at[t], sems.at[t]))
    for copy in copies:
        copy.wait()


def split_kernel(above, near, *halves):
    for n in range(2):
        halves[n][...] = above[n]
        halves[2 + n][...] = near[n]


def even_kernel(*refs):
    @pl.when(is_even())
    def _():
        post_body(((refs[:2], refs[2:4]), (refs[4:6], refs[6:8])), *refs[8:])


def odd_kernel(*refs):
    @pl.when(jnp.logical_not(is_even()))
    def _():
        post_body(((refs[:2], refs[2:4]), refs[4:6]), *refs[7:])


def local(clip, gain1, weight1, gain2, weight2, widths, links):
    tiles = lax.axis_size("tile")
    near_pairs = [(i, i ^ 1) for i in range(tiles)]
    odd_pairs = [(i + 1, i) for i in range(1, tiles - 1, 2)]
    cores = [(0, 1), (1, 0)]
    gain1, gain2 = gain1.reshape(1, C), gain2.reshape(1, C)
    clip, gain1, weight1, gain2, weight2 = (
        pltpu.with_memory_space_constraint(x, pltpu.HBM) for x in (clip, gain1, weight1, gain2, weight2)
    )
    edge = VM((2, BW, 4 * C), BF)
    weight = VM((3, 3, 3 * C, C), BF)
    clip, hidden, bottom, near, top, weight1, gain2, weight2 = pl.pallas_call(
        send_kernel,
        out_shape=(
            VM((4, 8, BW * C), BF), VM((4, 8, BW, L), BF), edge, edge, edge, weight, VM((1, C), F32), weight,
        ),
        in_specs=[hbm] * 5,
        out_specs=(vmem,) * 8,
        scratch_shapes=[VM((1, C), F32), VM((4, 8 * STEP, L), F32), DMA((8,))],
        compiler_params=PARAMS,
    )(clip, gain1, weight1, gain2, weight2)
    turn = tiles - FAR + CORNER
    ups = {i: i + 1 for i in range(tiles)} | {turn: 0, tiles - 1: turn + 1}
    above = lax.ppermute(bottom, "tile", list(ups.items()))
    near = lax.ppermute(near, "tile", near_pairs)
    earlier = lax.ppermute(hidden, "tm", cores)
    state = (
        VM((2, 9 * 256, 256), BF),
        VM((2, 9 * 256, 256), BF),
        VM((2, 6 * BW, 256), F32),
        VM((3, 8, 8, BW, L), BF),
        VM((3, 6, 6, BW, L), BF),
        VM((2, 4 * BW, 256), F32),
        VM((2, 4 * BW, 256), F32),
    )
    inputs = (hidden, earlier, weight1, gain2, weight2, widths)
    specs = [vmem] * 5 + [smem]
    top, *made = pl.pallas_call(
        early_kernel,
        out_shape=(edge, *state),
        in_specs=specs + [vmem],
        out_specs=(vmem,) * 8,
        input_output_aliases={6: 0},
        compiler_params=PARAMS,
    )(*inputs, top)
    other = lax.ppermute(top, "tile", odd_pairs)
    packed1, packed2, part1, _, x2 = pl.pallas_call(
        first_kernel,
        out_shape=state[:5],
        in_specs=specs + [vmem] * 5,
        out_specs=(vmem,) * 5,
        input_output_aliases={6 + n: n for n in range(5)},
        compiler_params=PARAMS,
    )(*inputs, *made[:5])
    above, near, x2 = lax.optimization_barrier((above, near, x2))
    half = VM((BW, 4 * C), BF)
    halves = pl.pallas_call(
        split_kernel,
        out_shape=(half,) * 4,
        in_specs=[vmem] * 2,
        out_specs=(vmem,) * 4,
        cost_estimate=SMALL,
        compiler_params=PARAMS,
    )(above, near)
    early_halves = [lax.ppermute(x, "tm", cores) for x in halves]
    above = (*early_halves[:2], *halves[:2])
    near = (*early_halves[2:], *halves[2:])
    part2, inner = pl.pallas_call(
        second_kernel,
        out_shape=state[5:],
        in_specs=[vmem] * 4,
        out_specs=(vmem,) * 2,
        input_output_aliases={2: 0, 3: 1},
        cost_estimate=SMALL,
        compiler_params=PARAMS,
    )(x2, packed2, *made[5:])
    early_other = lax.ppermute(other, "tm", cores)
    inputs = (clip, gain2, widths, links, packed1, packed2, part1, part2, inner)
    specs = [vmem] * 2 + [smem] + [vmem] * 6
    out = pltpu.HBM((4, 8, BW * C), BF)
    scratch = [
        VM((2, 3, 8, 2, BW, L), BF),
        VM((2, 3, 6, 2, BW, L), BF),
        VM((4, 8 * STEP, L), F32),
        VM((4, 8, BW * C), BF),
        DMA((4,)),
    ]
    done = pl.pallas_call(
        even_kernel,
        out_shape=out,
        in_specs=[vmem] * 8 + specs,
        out_specs=hbm,
        scratch_shapes=scratch,
        cost_estimate=LARGE,
        compiler_params=PARAMS,
    )(*above, *near, *inputs)
    return pl.pallas_call(
        odd_kernel,
        out_shape=out,
        in_specs=[vmem] * 6 + [hbm] + specs,
        out_specs=hbm,
        scratch_shapes=scratch,
        input_output_aliases={6: 0},
        compiler_params=PARAMS,
    )(*near, early_other, other, done, *inputs)


def solution(mesh):
    in_specs = (P("tm", "tile", None), P(), P(), P(), P(), P("tile"), P("tile", None))
    out_specs = P("tm", "tile", None)
    return jax.shard_map(local, mesh=mesh, in_specs=in_specs, out_specs=out_specs, check_vma=False)
```
